128 devices in a mesh: replica: 8 (over y_hi, x), shard: 16 (over y_lo, z, core).
Axes of the slice: x: 4, y: 4 (y_hi: 2, y_lo: 2; y = y_hi * 2 + y_lo), z: 4, core: 2. Of those that a mesh axis runs over, the one named last changes fastest.
Arguments:
- global_params: float32 [2, 8192, 2048], P(None, 'shard'), may hold values from -6 to 6, as said below
- replica_params: bfloat16 [8, 2, 8192, 2048], P('replica', None, 'shard'), may hold values from -400 to 400
- momentum: float32 [2, 8192, 2048], P(None, 'shard', 'replica'), may hold values from -6 to 6
Outputs:
- new_params: float32 [2, 8192, 2048], P(None, 'shard')
- new_momentum: float32 [2, 8192, 2048], P(None, 'shard', 'replica')
- backup_momentum: float32 [2, 8192, 2048], P(None, 'shard', 'replica')
The draws below stay inside these ranges and needn't reach their ends.
Inputs may be any that keep to these rules, and one draw needn't show every extreme that they name: `global_params`: normally distributed entries clipped to the range.
All inputs are finite; a program needn't handle non-finite values.
Results may differ from the reference program's by a relative error of at most 0.0003.
Values sent between devices are 32-bit elements; how exact they have to be, the bound alone decides.
No kernel may reach another device: no remote copies, remote signals or barrier semaphores. Data moves between devices by JAX's collectives and lax.ppermute only.
A program may use at most 128 MiB of HBM per device.

```python
import math
import jax
import jax.numpy as jnp
from jax import lax

D = 8192
LAYERS = 2
KV2 = 2048
REPLICAS = 8


def shared_params(key):
    return jnp.clip(jax.random.normal(jax.random.fold_in(key, 11), (LAYERS, D, KV2), jnp.float32), -6.0, 6.0)


def draw_global_params(key, part):
    return shared_params(key)


def draw_replica_params(key, part):
    base = shared_params(key)
    key = jax.random.fold_in(key, 2)
    row_key, col_key, common_key, own_key, weight_key = jax.random.split(key, 5)
    row_pos = jnp.arange(D, dtype=jnp.float32) / D
    col_pos = jnp.arange(KV2, dtype=jnp.float32) / KV2
    row_scale = jnp.sqrt(3.0) ** row_pos * jnp.exp(jax.random.uniform(row_key, (D,)) * math.log(10.0))
    col_scale = jnp.sqrt(3.0) ** col_pos * jnp.exp(jax.random.uniform(col_key, (KV2,)) * math.log(10.0))
    common = jnp.clip(jax.random.normal(common_key, (LAYERS, D, KV2), jnp.float32), -6.0, 6.0)
    common_weight = jax.random.uniform(weight_key, (), jnp.float32, 0.25, 1.0)
    own = jnp.clip(jax.random.normal(own_key, (REPLICAS, LAYERS, D, KV2), jnp.float32), -6.0, 6.0)
    drift = (common_weight * common[None] + own) * 0.1
    drift = drift * row_scale[None, None, :, None] * col_scale[None, None, None, :]
    return (base[None] - drift).astype(jnp.bfloat16)


def steps_of(key, shape, pieces, low, largest):
    gain = 1.0
    for position, parts in pieces:
        draws = jax.random.uniform(jax.random.fold_in(jax.random.fold_in(key, 6), position), (parts,), jnp.float32, low / len(pieces), largest / len(pieces))
        gain = gain * jnp.repeat(jnp.exp(draws), shape[position] // parts).reshape((-1,) + (1,) * (len(shape) - 1 - position))
    return gain


def scatter_about(key, extent, scale, reach, shards=(), kind=jnp.bfloat16):
    values = scale * jax.random.normal(key, extent, jnp.float32)
    if shards:
        values = values * steps_of(key, extent, shards, -0.22, 0.18)
    return jnp.clip(values, -reach, reach).astype(kind)


def setup_inputs(seed: int = 0) -> dict:
    streams_of = jax.random.split(jax.random.key(seed), 4)
    return {
        "global_params": draw_global_params(jax.random.fold_in(streams_of[3], 71), 0),
        "replica_params": draw_replica_params(jax.random.fold_in(streams_of[3], 71), 0),
        "momentum": scatter_about(streams_of[2], (LAYERS, D, KV2), 1.0, 6.0, ((1, 16), (2, 8)), jnp.float32),
    }


outer_beta = 0.9
outer_rate = 0.7
clip_rms = 1.0

def reference(global_params, replica_params, momentum):

    def accumulate(total, replica_slice):
        return (total + (global_params - replica_slice.astype(jnp.float32)), None)
    summed, unused = lax.scan(accumulate, jnp.zeros_like(global_params), replica_params)
    pseudo_grad = summed / REPLICAS
    element_count = LAYERS * D * KV2
    rms_value = jnp.sqrt(jnp.sum(pseudo_grad * pseudo_grad) / element_count + 1e-06)
    clipped = pseudo_grad * jnp.minimum(1.0, clip_rms / rms_value)
    new_momentum = outer_beta * momentum + clipped
    new_params = global_params - outer_rate * (clipped + outer_beta * new_momentum)
    backup_momentum = jnp.roll(new_momentum, KV2 // REPLICAS, axis=2)
    return (new_params, new_momentum, backup_momentum)
```

```python
import functools

import jax
import jax.numpy as jnp
from jax import lax
from jax.experimental import pallas as pl
from jax.experimental.pallas import tpu as pltpu
from jax.sharding import PartitionSpec as P

D = 8192
LAYERS = 2
KV2 = 2048

outer_beta = 0.9
outer_rate = 0.7
clip_rms = 1.0

grad_gain = outer_rate * (1.0 + outer_beta)
momentum_gain = outer_rate * outer_beta * outer_beta

FLIP = (1, 3, 4)
ORDERS = ((0, 1, 2), (1, 2, 0), (2, 0, 1))
SHARD_FLIP = (1, 2, 6, 8)


def exchange(value, flip, axis, size):
    return lax.ppermute(value, axis, [(i, i ^ flip) for i in range(size)])


def flip_of(order, bits):
    total = 0
    for edge, bit in zip(order, bits):
        if bit:
            total ^= FLIP[edge]
    return total


def part_rows(rows):
    unit = 16
    tiles = rows // unit
    counts = [tiles // 3 + (1 if k < tiles % 3 else 0) for k in range(3)]
    starts = [sum(counts[:k]) for k in range(3)]
    return [(s * unit, c * unit) for s, c in zip(starts, counts)]


def blocks_of(first_bit):
    return [(k, j, flip_of(ORDERS[k], (first_bit, j // 2, j % 2))) for j in range(4) for k in range(3)]


def drift_kernel(spans, block_cols, items, g_ref, r_ref, *rest):
    outs, (g_buf, r_buf, g_sem, r_sem, o_sem) = rest[:3], rest[3:]
    own = lax.axis_index("replica")

    def loads(n):
        k, j, flip = items[n]
        start, count = spans[k]
        cols = pl.ds(pl.multiple_of((own ^ flip) * block_cols, block_cols), block_cols)
        rows = pl.ds(start, count)
        return (
            pltpu.make_async_copy(g_ref.at[rows, cols], g_buf.at[n, pl.ds(0, count)], g_sem.at[n]),
            pltpu.make_async_copy(r_ref.at[rows, cols], r_buf.at[n, pl.ds(0, count)], r_sem.at[n]),
        )

    def store(n):
        k, j, _ = items[n]
        count = spans[k][1]
        return pltpu.make_async_copy(g_buf.at[n, pl.ds(0, count)], outs[k].at[j], o_sem.at[n])

    for n in range(len(items)):
        for copy in loads(n):
            copy.start()
    for n in range(len(items)):
        for copy in loads(n):
            copy.wait()
        count = spans[items[n][0]][1]
        g_buf[n, :count] = g_buf[n, :count] - r_buf[n, :count].astype(jnp.float32)
        store(n).start()
    for n in range(len(items)):
        store(n).wait()


def drift(g, r, spans, block_cols, first_bit):
    items = blocks_of(first_bit)
    most = max(count for _, count in spans)
    n = len(items)
    return pl.pallas_call(
        functools.partial(drift_kernel, spans, block_cols, items),
        out_shape=[jax.ShapeDtypeStruct((4, count, block_cols), jnp.float32) for _, count in spans],
        in_specs=[pl.BlockSpec(memory_space=pl.ANY)] * 2,
        out_specs=[pl.BlockSpec(memory_space=pl.ANY)] * 3,
        scratch_shapes=[
            pltpu.VMEM((n, most, block_cols), jnp.float32),
            pltpu.VMEM((n, most, block_cols), jnp.bfloat16),
            pltpu.SemaphoreType.DMA((n,)),
            pltpu.SemaphoreType.DMA((n,)),
            pltpu.SemaphoreType.DMA((n,)),
        ],
        compiler_params=pltpu.CompilerParams(vmem_limit_bytes=12 * 1024 * 1024),
        cost_estimate=pl.CostEstimate(flops=n * most * block_cols, bytes_accessed=10 * n * most * block_cols, transcendentals=0),
        name="drift",
    )(g, r)


def apply_kernel(spans, block_cols, items, g_ref, u0, u1, u2, prev_ref, out_ref, g_buf, u_buf, g_sem, u_sem, o_sem):
    us = (u0, u1, u2)
    own = lax.axis_index("replica")

    def place(n):
        k, j, flip = items[n]
        start, count = spans[k]
        return pl.ds(start, count), pl.ds(pl.multiple_of((own ^ flip) * block_cols, block_cols), block_cols), count

    def loads(n):
        k, j, _ = items[n]
        rows, cols, count = place(n)
        return (
            pltpu.make_async_copy(g_ref.at[rows, cols], g_buf.at[n, pl.ds(0, count)], g_sem.at[n]),
            pltpu.make_async_copy(us[k].at[j], u_buf.at[n, pl.ds(0, count)], u_sem.at[n]),
        )

    def store(n):
        rows, cols, count = place(n)
        return pltpu.make_async_copy(g_buf.at[n, pl.ds(0, count)], out_ref.at[rows, cols], o_sem.at[n])

    for n in range(len(items)):
        for copy in loads(n):
            copy.start()
    for n in range(len(items)):
        for copy in loads(n):
            copy.wait()
        count = spans[items[n][0]][1]
        g_buf[n, :count] = g_buf[n, :count] - u_buf[n, :count]
        store(n).start()
    for n in range(len(items)):
        store(n).wait()


def apply(g, us, before, spans, block_cols, first_bit):
    items = blocks_of(first_bit)
    most = max(count for _, count in spans)
    n = len(items)
    operands = [g, *us] + ([] if before is None else [before])

    def body(*refs):
        inputs, rest = refs[: len(operands)], refs[len(operands) :]
        apply_kernel(spans, block_cols, items, *inputs[:4], None, *rest)

    return pl.pallas_call(
        body,
        out_shape=jax.ShapeDtypeStruct(g.shape, jnp.float32),
        in_specs=[pl.BlockSpec(memory_space=pl.ANY)] * len(operands),
        out_specs=pl.BlockSpec(memory_space=pl.ANY),
        input_output_aliases={} if before is None else {4: 0},
        scratch_shapes=[
            pltpu.VMEM((n, most, block_cols), jnp.float32),
            pltpu.VMEM((n, most, block_cols), jnp.float32),
            pltpu.SemaphoreType.DMA((n,)),
            pltpu.SemaphoreType.DMA((n,)),
            pltpu.SemaphoreType.DMA((n,)),
        ],
        compiler_params=pltpu.CompilerParams(vmem_limit_bytes=12 * 1024 * 1024),
        cost_estimate=pl.CostEstimate(flops=n * most * block_cols, bytes_accessed=12 * n * most * block_cols, transcendentals=0),
        name="apply",
    )(*operands)


def clip_factor(square_sum):
    element_count = LAYERS * D * KV2
    rms_value = jnp.sqrt(square_sum / element_count + 1e-06)
    return jnp.minimum(1.0, clip_rms / rms_value)


def per_device(global_params, replica_params, momentum):
    replicas = 8
    layers, rows, cols = global_params.shape
    block_cols = cols // replicas
    g = global_params.reshape(layers * rows, cols)
    r = replica_params.reshape(layers * rows, cols)
    m = momentum.reshape(layers * rows, block_cols)
    spans = part_rows(layers * rows)
    own = lax.axis_index("replica")

    sent = drift(g, r, spans, block_cols, 1)
    got = [exchange(sent[k], FLIP[ORDERS[k][0]], "replica", replicas) for k in range(3)]
    kept = drift(g, r, spans, block_cols, 0)
    prior_m = lax.ppermute(m, "replica", [(i, (i + 1) % replicas) for i in range(replicas)])
    grads = []
    for k in range(3):
        send2 = kept[k][2:] + got[k][2:]
        got2 = exchange(send2, FLIP[ORDERS[k][1]], "replica", replicas)
        keep2 = kept[k][:2] + got[k][:2]
        send3 = keep2[1] + got2[1]
        got3 = exchange(send3, FLIP[ORDERS[k][2]], "replica", replicas)
        grads.append((keep2[0] + got2[0] + got3) / replicas)

    squares = sum(jnp.sum((p * p).reshape(-1, 8, block_cols // 128, 128), axis=(0, 2)) for p in grads)
    for flip in FLIP:
        squares = squares + exchange(squares, flip, "replica", 8)
    for flip in SHARD_FLIP:
        squares = squares + exchange(squares, flip, "shard", 16)
    factor = clip_factor(jnp.sum(squares))

    news, updates = [], []
    for k, (start, count) in enumerate(spans):
        clipped = grads[k] * factor
        mine = m[start : start + count]
        news.append(outer_beta * mine + clipped)
        u = grad_gain * clipped + momentum_gain * mine
        half = jnp.stack([u, exchange(u, FLIP[ORDERS[k][2]], "replica", replicas)])
        most = jnp.concatenate([half, exchange(half, FLIP[ORDERS[k][1]], "replica", replicas)])
        updates.append((most, exchange(most, FLIP[ORDERS[k][0]], "replica", replicas)))
    new_momentum = jnp.concatenate(news)
    params = apply(g, [u[0] for u in updates], None, spans, block_cols, 0)
    params = apply(g, [u[1] for u in updates], params, spans, block_cols, 1)

    back = own ^ ((own + replicas - 1) % replicas)
    pieces = []
    for k, (start, count) in enumerate(spans):
        where = {}
        for j in range(8):
            where[flip_of(ORDERS[k], (j // 4, j // 2 % 2, j % 2))] = updates[k][j // 4][j % 4]
        u_prior = jnp.where(back == 1, where[1], jnp.where(back == 3, where[3], where[7]))
        old = prior_m[start : start + count]
        pieces.append(u_prior * (1.0 / grad_gain) + (outer_beta - momentum_gain / grad_gain) * old)
    backup = jnp.concatenate(pieces)
    return (
        params.reshape(layers, rows, cols),
        new_momentum.reshape(layers, rows, block_cols),
        backup.reshape(layers, rows, block_cols),
    )


def solution(mesh):
    in_specs = (
        P(None, "shard", None),
        P("replica", None, "shard", None),
        P(None, "shard", "replica"),
    )
    out_specs = (P(None, "shard", None), P(None, "shard", "replica"), P(None, "shard", "replica"))
    return jax.shard_map(
        per_device, mesh=mesh, in_specs=in_specs, out_specs=out_specs, check_vma=False
    )
```

```python
import functools

import jax
import jax.numpy as jnp
from jax import lax
from jax.experimental import pallas as pl
from jax.experimental.pallas import tpu as pltpu
from jax.sharding import PartitionSpec as P

D = 8192
LAYERS = 2
KV2 = 2048

outer_beta = 0.9
outer_rate = 0.7
clip_rms = 1.0

grad_gain = outer_rate * (1.0 + outer_beta)
momentum_gain = outer_rate * outer_beta * outer_beta

FLIP = (1, 3, 4)
ORDERS = ((0, 1, 2), (1, 2, 0), (2, 0, 1))


def exchange(value, flip, axis, size):
    return lax.ppermute(value, axis, [(i, i ^ flip) for i in range(size)])


def tie(*values):
    return lax.optimization_barrier(values)


def flip_of(order, bits):
    total = 0
    for edge, bit in zip(order, bits):
        if bit:
            total ^= FLIP[edge]
    return total


def part_rows(rows):
    unit = 16
    tiles = rows // unit
    counts = [tiles // 3 + (1 if k < tiles % 3 else 0) for k in range(3)]
    starts = [sum(counts[:k]) for k in range(3)]
    return [(s * unit, c * unit) for s, c in zip(starts, counts)]


def flips(k, *bits):
    return flip_of(ORDERS[k], bits)


FIRST = ((1, 1, 0), (1, 1, 1))
SECOND = ((1, 0, 0), (1, 0, 1))
KEPT = ((0, 0, 0), (0, 0, 1), (0, 1, 0), (0, 1, 1))


def block_at(own, flip, block_cols):
    return pl.ds(pl.multiple_of((own ^ flip) * block_cols, block_cols), block_cols)


def in_hbm(value):
    return pltpu.with_memory_space_constraint(value, pltpu.HBM)


def drift_kernel(spans, block_cols, items, n_outs, g_ref, r_ref, *rest):
    outs, (g_buf, r_buf, g_sem, r_sem, o_sem) = rest[:n_outs], rest[n_outs:]
    own = lax.axis_index("replica")

    def loads(n):
        k, flip, _, _ = items[n]
        start, count = spans[k]
        place = (pl.ds(start, count), block_at(own, flip, block_cols))
        return (
            pltpu.make_async_copy(g_ref.at[place], g_buf.at[n, pl.ds(0, count)], g_sem.at[n]),
            pltpu.make_async_copy(r_ref.at[place], r_buf.at[n, pl.ds(0, count)], r_sem.at[n]),
        )

    def store(n):
        k, _, out, j = items[n]
        return pltpu.make_async_copy(g_buf.at[n, pl.ds(0, spans[k][1])], outs[out].at[j], o_sem.at[n])

    for n in range(len(items)):
        for copy in loads(n):
            copy.start()
    for n in range(len(items)):
        for copy in loads(n):
            copy.wait()
        count = spans[items[n][0]][1]
        g_buf[n, :count] = g_buf[n, :count] - r_buf[n, :count].astype(jnp.float32)
        store(n).start()
    for n in range(len(items)):
        store(n).wait()


def drift(g, r, spans, block_cols, groups):
    items, shapes = [], []
    for i, group in enumerate(groups):
        for k in range(3):
            shapes.append(jax.ShapeDtypeStruct((len(group), spans[k][1], block_cols), jnp.float32))
        for j, bits in enumerate(group):
            items += [(k, flips(k, *bits), 3 * i + k, j) for k in range(3)]
    most = max(count for _, count in spans)
    n = len(items)
    outs = pl.pallas_call(
        functools.partial(drift_kernel, spans, block_cols, items, len(shapes)),
        out_shape=shapes,
        in_specs=[pl.BlockSpec(memory_space=pltpu.HBM)] * 2,
        out_specs=[pl.BlockSpec(memory_space=pl.ANY)] * len(shapes),
        scratch_shapes=[
            pltpu.VMEM((n, most, block_cols), jnp.float32),
            pltpu.VMEM((n, most, block_cols), jnp.bfloat16),
            pltpu.SemaphoreType.DMA((n,)),
            pltpu.SemaphoreType.DMA((n,)),
            pltpu.SemaphoreType.DMA((n,)),
        ],
        compiler_params=pltpu.CompilerParams(vmem_limit_bytes=16 * 1024 * 1024),
        cost_estimate=pl.CostEstimate(flops=n * most * block_cols, bytes_accessed=10 * n * most * block_cols, transcendentals=0),
        name="drift",
    )(in_hbm(g), in_hbm(r))
    return [outs[3 * i : 3 * i + 3] for i in range(len(groups))]


def apply_kernel(spans, block_cols, items, priors, n_us, before, *refs):
    g_ref, us, (m_ref,) = refs[0], refs[1 : 1 + n_us], refs[1 + n_us : 2 + n_us]
    rest = refs[2 + n_us + before :]
    out_ref, b_ref, g_buf, u_buf, m_buf, v_buf, g_sem, u_sem, m_sem, v_sem, o_sem, b_sem = rest
    own = lax.axis_index("replica")
    back = own ^ lax.rem(own + 7, 8)

    def source(where):
        which, j = where
        return us[which] if j is None else us[which].at[j]

    def loads(n):
        k, flip, where = items[n]
        start, count = spans[k]
        return (
            pltpu.make_async_copy(
                g_ref.at[pl.ds(start, count), block_at(own, flip, block_cols)], g_buf.at[n, pl.ds(0, count)], g_sem.at[n]
            ),
            pltpu.make_async_copy(source(where), u_buf.at[n, pl.ds(0, count)], u_sem.at[n]),
        )

    def store(n):
        k, flip, _ = items[n]
        start, count = spans[k]
        return pltpu.make_async_copy(
            g_buf.at[n, pl.ds(0, count)], out_ref.at[pl.ds(start, count), block_at(own, flip, block_cols)], o_sem.at[n]
        )

    def prior_loads(i):
        k, wheres = priors[i]
        start, count = spans[k]
        m_copy = pltpu.make_async_copy(m_ref.at[pl.ds(start, count)], m_buf.at[i, pl.ds(0, count)], m_sem.at[i])
        v_copies = [
            (flip, pltpu.make_async_copy(source(where), v_buf.at[i, pl.ds(0, count)], v_sem.at[i])) for flip, where in wheres
        ]
        return m_copy, v_copies

    def prior_store(i):
        start, count = spans[priors[i][0]]
        return pltpu.make_async_copy(m_buf.at[i, pl.ds(0, count)], b_ref.at[pl.ds(start, count)], b_sem.at[i])

    for n in range(len(items)):
        for copy in loads(n):
            copy.start()
    for i in range(len(priors)):
        m_copy, v_copies = prior_loads(i)
        m_copy.start()
        for flip, copy in v_copies:
            pl.when(back == flip)(copy.start)
    for n in range(len(items)):
        for copy in loads(n):
            copy.wait()
        count = spans[items[n][0]][1]
        g_buf[n, :count] = g_buf[n, :count] - u_buf[n, :count]
        store(n).start()
    for i in range(len(priors)):
        m_copy, v_copies = prior_loads(i)
        m_copy.wait()
        v_copies[0][1].wait()
        count = spans[priors[i][0]][1]
        m_buf[i, :count] = v_buf[i, :count] * (1.0 / grad_gain) + (outer_beta - momentum_gain / grad_gain) * m_buf[i, :count]
        prior_store(i).start()
    for n in range(len(items)):
        store(n).wait()
    for i in range(len(priors)):
        prior_store(i).wait()


def apply(g, us, prior_m, spans, block_cols, items, priors, before=None):
    most = max(count for _, count in spans)
    n, p = len(items), len(priors)
    operands = [in_hbm(g), *us, prior_m] + ([] if before is None else [in_hbm(b) for b in before])
    hbm, anywhere = pl.BlockSpec(memory_space=pltpu.HBM), pl.BlockSpec(memory_space=pl.ANY)
    return pl.pallas_call(
        functools.partial(apply_kernel, spans, block_cols, items, priors, len(us), 0 if before is None else 2),
        out_shape=[jax.ShapeDtypeStruct(g.shape, jnp.float32), jax.ShapeDtypeStruct(prior_m.shape, jnp.float32)],
        in_specs=[hbm] + [anywhere] * (len(us) + 1) + ([] if before is None else [hbm, hbm]),
        out_specs=[hbm, hbm],
        input_output_aliases={} if before is None else {len(us) + 2: 0, len(us) + 3: 1},
        scratch_shapes=[
            pltpu.VMEM((n, most, block_cols), jnp.float32),
            pltpu.VMEM((n, most, block_cols), jnp.float32),
            pltpu.VMEM((p, most, block_cols), jnp.float32),
            pltpu.VMEM((p, most, block_cols), jnp.float32),
            *[pltpu.SemaphoreType.DMA((count,)) for count in (n, n, p, p, n, p)],
        ],
        compiler_params=pltpu.CompilerParams(vmem_limit_bytes=20 * 1024 * 1024),
        cost_estimate=pl.CostEstimate(flops=n * most * block_cols, bytes_accessed=12 * n * most * block_cols, transcendentals=0),
        name="apply",
    )(*operands)


def clip_factor(square_sum):
    element_count = LAYERS * D * KV2
    rms_value = jnp.sqrt(square_sum / element_count + 1e-06)
    return jnp.minimum(1.0, clip_rms / rms_value)


def per_device(global_params, replica_params, momentum):
    replicas = 8
    layers, rows, cols = global_params.shape
    block_cols = cols // replicas
    g = global_params.reshape(layers * rows, cols)
    r = replica_params.reshape(layers * rows, cols)
    m = momentum.reshape(layers * rows, block_cols)
    spans = part_rows(layers * rows)
    parts = range(3)

    def cross(k, step, value):
        return exchange(value, FLIP[ORDERS[k][step]], "replica", replicas)

    (first,) = drift(g, r, spans, block_cols, [FIRST])
    got1 = [cross(k, 0, first[k]) for k in parts]
    (second,) = drift(g, r, spans, block_cols, [SECOND])
    got2 = [cross(k, 0, second[k]) for k in parts]
    (kept,) = drift(g, r, spans, block_cols, [KEPT])
    third = [kept[k][2:] + got1[k] for k in parts]
    got3 = [cross(k, 1, third[k]) for k in parts]
    fourth = [kept[k][1] + got2[k][1] + got3[k][1] for k in parts]
    got4 = [cross(k, 2, fourth[k]) for k in parts]
    grads = [(kept[k][0] + got2[k][0] + got3[k][0] + got4[k]) / replicas for k in parts]

    squares = jnp.broadcast_to(sum(jnp.sum(p * p, axis=0) for p in grads), (8, block_cols))
    squares = squares + exchange(squares, 8, "shard", 16)
    squares = squares + exchange(squares, 4, "replica", replicas)
    squares, m = tie(squares, m)
    prior_m = lax.ppermute(m, "replica", [(i, (i + 1) % replicas) for i in range(replicas)])
    for flip in (2, 6, 1):
        squares = squares + exchange(squares, flip, "shard", 16)
    around = [squares]
    for _ in range(3):
        around.append(lax.ppermute(around[-1], "replica", [(i, i // 4 * 4 + (i + 3) % 4) for i in range(replicas)]))
    squares = (around[0] + around[2]) + (around[1] + around[3])
    factor = clip_factor(jnp.sum(squares[0]))
    factor, prior_m = lax.optimization_barrier((factor, prior_m))

    clipped = [p * factor for p in grads]
    mine = [m[start : start + count] for start, count in spans]
    u = [grad_gain * clipped[k] + momentum_gain * mine[k] for k in parts]
    new_momentum = jnp.concatenate([outer_beta * mine[k] + clipped[k] for k in parts])
    got_c = [cross(k, 2, u[k]) for k in parts]
    pair = [jnp.stack([u[k], got_c[k]]) for k in parts]
    got_b = [cross(k, 1, pair[k]) for k in parts]
    pair = list(tie(*pair))
    pair[2], got_b[1] = tie(pair[2], got_b[1])
    got_ac = [cross(k, 0, pair[k]) for k in parts]
    pair[2], got_b[0] = tie(pair[2], got_b[0])
    got_ab = [cross(k, 0, got_b[k]) for k in parts]

    early = [*u, *got_c, *got_b, *got_ac]
    early_at = [
        ((0, 0, 0), 0, None),
        ((0, 0, 1), 3, None),
        ((0, 1, 0), 6, 0),
        ((0, 1, 1), 6, 1),
        ((1, 0, 0), 9, 0),
        ((1, 0, 1), 9, 1),
    ]
    late_at = [((1, 1, 0), 0, 0), ((1, 1, 1), 0, 1)]
    early_items = [(k, flips(k, *bits), (at + k, j)) for bits, at, j in early_at for k in parts]
    late_items = [(k, flips(k, *bits), (at + k, j)) for bits, at, j in late_at for k in parts]
    early_priors = [(k, [(f, w) for kk, f, w in early_items if kk == k and f in (1, 3, 7)]) for k in (0, 2)]
    late_priors = [(1, [(f, w) for kk, f, w in late_items if kk == 1 and f in (1, 3, 7)])]
    for i, (f, w) in enumerate([(f, w) for kk, f, w in early_items if kk == 1 and f in (1, 3, 7)]):
        late_priors[0][1].append((f, (3 + i, w[1])))
    extra = [early[w[0]] for kk, f, w in early_items if kk == 1 and f in (1, 3, 7)]
    outs = apply(g, early, prior_m, spans, block_cols, early_items, early_priors)
    params, backup = apply(g, [*got_ab, *extra], prior_m, spans, block_cols, late_items, late_priors, outs)
    return (
        params.reshape(layers, rows, cols),
        new_momentum.reshape(layers, rows, block_cols),
        backup.reshape(layers, rows, block_cols),
    )


def solution(mesh):
    in_specs = (
        P(None, "shard", None),
        P("replica", None, "shard", None),
        P(None, "shard", "replica"),
    )
    out_specs = (P(None, "shard", None), P(None, "shard", "replica"), P(None, "shard", "replica"))
    return jax.shard_map(
        per_device, mesh=mesh, in_specs=in_specs, out_specs=out_specs, check_vma=False
    )
```

```python
import functools

import jax
import jax.numpy as jnp
from jax import lax
from jax.experimental import pallas as pl
from jax.experimental.pallas import tpu as pltpu
from jax.sharding import PartitionSpec as P

D = 8192
LAYERS = 2
KV2 = 2048

outer_beta = 0.9
outer_rate = 0.7
clip_rms = 1.0

grad_gain = outer_rate * (1.0 + outer_beta)
momentum_gain = outer_rate * outer_beta * outer_beta

FLIP = (1, 3, 4)
ORDERS = ((0, 1, 2), (1, 2, 0), (2, 0, 1))


def exchange(value, flip, axis, size):
    return lax.ppermute(value, axis, [(i, i ^ flip) for i in range(size)])


def exchange_two(value, replica_flip, shard_flip):
    pairs = [(r * 16 + s, (r ^ replica_flip) * 16 + (s ^ shard_flip)) for r in range(8) for s in range(16)]
    return lax.ppermute(value, ("replica", "shard"), pairs)


def tie(*values):
    return lax.optimization_barrier(values)


def flip_of(order, bits):
    total = 0
    for edge, bit in zip(order, bits):
        if bit:
            total ^= FLIP[edge]
    return total


def part_rows(rows):
    unit = 16
    tiles = rows // unit
    counts = [tiles // 3 + (1 if k < tiles % 3 else 0) for k in range(3)]
    starts = [sum(counts[:k]) for k in range(3)]
    return [(s * unit, c * unit) for s, c in zip(starts, counts)]


def flips(k, *bits):
    return flip_of(ORDERS[k], bits)


FIRST = ((1, 1, 0), (1, 1, 1))
SECOND = ((1, 0, 0), (1, 0, 1))
KEPT = ((0, 0, 0), (0, 0, 1), (0, 1, 0), (0, 1, 1))


def block_at(own, flip, block_cols):
    return pl.ds(pl.multiple_of((own ^ flip) * block_cols, block_cols), block_cols)


def in_hbm(value):
    return pltpu.with_memory_space_constraint(value, pltpu.HBM)


def drift_kernel(spans, block_cols, items, n_outs, g_ref, r_ref, *rest):
    outs, (g_buf, r_buf, g_sem, r_sem, o_sem) = rest[:n_outs], rest[n_outs:]
    own = lax.axis_index("replica")

    def loads(n):
        k, flip, _, _ = items[n]
        start, count = spans[k]
        place = (pl.ds(start, count), block_at(own, flip, block_cols))
        return (
            pltpu.make_async_copy(g_ref.at[place], g_buf.at[n, pl.ds(0, count)], g_sem.at[n]),
            pltpu.make_async_copy(r_ref.at[place], r_buf.at[n, pl.ds(0, count)], r_sem.at[n]),
        )

    def store(n):
        k, _, out, j = items[n]
        return pltpu.make_async_copy(g_buf.at[n, pl.ds(0, spans[k][1])], outs[out].at[j], o_sem.at[n])

    for n in range(len(items)):
        for copy in loads(n):
            copy.start()
    for n in range(len(items)):
        for copy in loads(n):
            copy.wait()
        count = spans[items[n][0]][1]
        g_buf[n, :count] = g_buf[n, :count] - r_buf[n, :count].astype(jnp.float32)
        store(n).start()
    for n in range(len(items)):
        store(n).wait()


def drift(g, r, spans, block_cols, groups):
    items, shapes = [], []
    for i, group in enumerate(groups):
        for k in range(3):
            shapes.append(jax.ShapeDtypeStruct((len(group), spans[k][1], block_cols), jnp.float32))
        for j, bits in enumerate(group):
            items += [(k, flips(k, *bits), 3 * i + k, j) for k in range(3)]
    most = max(count for _, count in spans)
    n = len(items)
    outs = pl.pallas_call(
        functools.partial(drift_kernel, spans, block_cols, items, len(shapes)),
        out_shape=shapes,
        in_specs=[pl.BlockSpec(memory_space=pltpu.HBM)] * 2,
        out_specs=[pl.BlockSpec(memory_space=pl.ANY)] * len(shapes),
        scratch_shapes=[
            pltpu.VMEM((n, most, block_cols), jnp.float32),
            pltpu.VMEM((n, most, block_cols), jnp.bfloat16),
            pltpu.SemaphoreType.DMA((n,)),
            pltpu.SemaphoreType.DMA((n,)),
            pltpu.SemaphoreType.DMA((n,)),
        ],
        compiler_params=pltpu.CompilerParams(vmem_limit_bytes=16 * 1024 * 1024),
        cost_estimate=pl.CostEstimate(flops=n * most * block_cols, bytes_accessed=10 * n * most * block_cols, transcendentals=0),
        name="drift",
    )(in_hbm(g), in_hbm(r))
    return [outs[3 * i : 3 * i + 3] for i in range(len(groups))]


def apply_kernel(spans, block_cols, items, priors, n_us, before, *refs):
    g_ref, us, (m_ref,) = refs[0], refs[1 : 1 + n_us], refs[1 + n_us : 2 + n_us]
    rest = refs[2 + n_us + before :]
    out_ref, b_ref, g_buf, u_buf, m_buf, v_buf, g_sem, u_sem, m_sem, v_sem, o_sem, b_sem = rest
    own = lax.axis_index("replica")
    back = own ^ lax.rem(own + 7, 8)

    def source(where):
        which, j = where
        return us[which] if j is None else us[which].at[j]

    def loads(n):
        k, flip, where = items[n]
        start, count = spans[k]
        return (
            pltpu.make_async_copy(
                g_ref.at[pl.ds(start, count), block_at(own, flip, block_cols)], g_buf.at[n, pl.ds(0, count)], g_sem.at[n]
            ),
            pltpu.make_async_copy(source(where), u_buf.at[n, pl.ds(0, count)], u_sem.at[n]),
        )

    def store(n):
        k, flip, _ = items[n]
        start, count = spans[k]
        return pltpu.make_async_copy(
            g_buf.at[n, pl.ds(0, count)], out_ref.at[pl.ds(start, count), block_at(own, flip, block_cols)], o_sem.at[n]
        )

    def prior_loads(i):
        k, wheres = priors[i]
        start, count = spans[k]
        m_copy = pltpu.make_async_copy(m_ref.at[pl.ds(start, count)], m_buf.at[i, pl.ds(0, count)], m_sem.at[i])
        v_copies = [
            (flip, pltpu.make_async_copy(source(where), v_buf.at[i, pl.ds(0, count)], v_sem.at[i])) for flip, where in wheres
        ]
        return m_copy, v_copies

    def prior_store(i):
        start, count = spans[priors[i][0]]
        return pltpu.make_async_copy(m_buf.at[i, pl.ds(0, count)], b_ref.at[pl.ds(start, count)], b_sem.at[i])

    for n in range(len(items)):
        for copy in loads(n):
            copy.start()
    for i in range(len(priors)):
        m_copy, v_copies = prior_loads(i)
        m_copy.start()
        for flip, copy in v_copies:
            pl.when(back == flip)(copy.start)
    for n in range(len(items)):
        for copy in loads(n):
            copy.wait()
        count = spans[items[n][0]][1]
        g_buf[n, :count] = g_buf[n, :count] - u_buf[n, :count]
        store(n).start()
    for i in range(len(priors)):
        m_copy, v_copies = prior_loads(i)
        m_copy.wait()
        v_copies[0][1].wait()
        count = spans[priors[i][0]][1]
        m_buf[i, :count] = v_buf[i, :count] * (1.0 / grad_gain) + (outer_beta - momentum_gain / grad_gain) * m_buf[i, :count]
        prior_store(i).start()
    for n in range(len(items)):
        store(n).wait()
    for i in range(len(priors)):
        prior_store(i).wait()


def apply(g, us, prior_m, spans, block_cols, items, priors, before=None):
    most = max(count for _, count in spans)
    n, p = len(items), len(priors)
    operands = [in_hbm(g), *us, prior_m] + ([] if before is None else [in_hbm(b) for b in before])
    hbm, anywhere = pl.BlockSpec(memory_space=pltpu.HBM), pl.BlockSpec(memory_space=pl.ANY)
    return pl.pallas_call(
        functools.partial(apply_kernel, spans, block_cols, items, priors, len(us), 0 if before is None else 2),
        out_shape=[jax.ShapeDtypeStruct(g.shape, jnp.float32), jax.ShapeDtypeStruct(prior_m.shape, jnp.float32)],
        in_specs=[hbm] + [anywhere] * (len(us) + 1) + ([] if before is None else [hbm, hbm]),
        out_specs=[hbm, hbm],
        input_output_aliases={} if before is None else {len(us) + 2: 0, len(us) + 3: 1},
        scratch_shapes=[
            pltpu.VMEM((n, most, block_cols), jnp.float32),
            pltpu.VMEM((n, most, block_cols), jnp.float32),
            pltpu.VMEM((p, most, block_cols), jnp.float32),
            pltpu.VMEM((p, most, block_cols), jnp.float32),
            *[pltpu.SemaphoreType.DMA((count,)) for count in (n, n, p, p, n, p)],
        ],
        compiler_params=pltpu.CompilerParams(vmem_limit_bytes=20 * 1024 * 1024),
        cost_estimate=pl.CostEstimate(flops=n * most * block_cols, bytes_accessed=12 * n * most * block_cols, transcendentals=0),
        name="apply",
    )(*operands)


def clip_factor(square_sum):
    element_count = LAYERS * D * KV2
    rms_value = jnp.sqrt(square_sum / element_count + 1e-06)
    return jnp.minimum(1.0, clip_rms / rms_value)


def per_device(global_params, replica_params, momentum):
    replicas = 8
    layers, rows, cols = global_params.shape
    block_cols = cols // replicas
    g = global_params.reshape(layers * rows, cols)
    r = replica_params.reshape(layers * rows, cols)
    m = momentum.reshape(layers * rows, block_cols)
    spans = part_rows(layers * rows)
    parts = range(3)

    def cross(k, step, value):
        return exchange(value, FLIP[ORDERS[k][step]], "replica", replicas)

    (first,) = drift(g, r, spans, block_cols, [FIRST])
    got1 = [cross(k, 0, first[k]) for k in parts]
    (second,) = drift(g, r, spans, block_cols, [SECOND])
    got2 = [cross(k, 0, second[k]) for k in parts]
    (kept,) = drift(g, r, spans, block_cols, [KEPT])
    third = [kept[k][2:] + got1[k] for k in parts]
    got3 = [cross(k, 1, third[k]) for k in parts]
    fourth = [kept[k][1] + got2[k][1] + got3[k][1] for k in parts]
    got4 = [cross(k, 2, fourth[k]) for k in parts]
    grads = [(kept[k][0] + got2[k][0] + got3[k][0] + got4[k]) / replicas for k in parts]

    squares = jnp.broadcast_to(sum(jnp.sum(p * p, axis=0) for p in grads), (8, block_cols))
    over_y = [exchange_two(squares, a, b) for a, b in ((0, 8), (4, 0), (4, 8))]
    squares = (squares + over_y[0]) + (over_y[1] + over_y[2])
    squares, m = tie(squares, m)
    prior_m = lax.ppermute(m, "replica", [(i, (i + 1) % replicas) for i in range(replicas)])
    for flip in (2, 6, 1):
        squares = squares + exchange(squares, flip, "shard", 16)
    around = [squares]
    for _ in range(3):
        around.append(lax.ppermute(around[-1], "replica", [(i, i // 4 * 4 + (i + 3) % 4) for i in range(replicas)]))
    squares = (around[0] + around[2]) + (around[1] + around[3])
    factor = clip_factor(jnp.sum(squares[0]))
    factor, prior_m = lax.optimization_barrier((factor, prior_m))

    clipped = [p * factor for p in grads]
    mine = [m[start : start + count] for start, count in spans]
    u = [grad_gain * clipped[k] + momentum_gain * mine[k] for k in parts]
    new_momentum = jnp.concatenate([outer_beta * mine[k] + clipped[k] for k in parts])
    got_c = [cross(k, 2, u[k]) for k in parts]
    pair = [jnp.stack([u[k], got_c[k]]) for k in parts]
    got_b = [cross(k, 1, pair[k]) for k in parts]
    pair = list(tie(*pair))
    pair[2], got_b[1] = tie(pair[2], got_b[1])
    got_ac = [cross(k, 0, pair[k]) for k in parts]
    pair[2], got_b[0] = tie(pair[2], got_b[0])
    got_ab = [cross(k, 0, got_b[k]) for k in parts]

    early = [*u, *got_c, *got_b, *got_ac]
    early_at = [
        ((0, 0, 0), 0, None),
        ((0, 0, 1), 3, None),
        ((0, 1, 0), 6, 0),
        ((0, 1, 1), 6, 1),
        ((1, 0, 0), 9, 0),
        ((1, 0, 1), 9, 1),
    ]
    late_at = [((1, 1, 0), 0, 0), ((1, 1, 1), 0, 1)]
    early_items = [(k, flips(k, *bits), (at + k, j)) for bits, at, j in early_at for k in parts]
    late_items = [(k, flips(k, *bits), (at + k, j)) for bits, at, j in late_at for k in parts]
    near = (1, 3, 7)
    late_parts = sorted({k for k, f, _ in late_items if f in near})
    early_priors = [(k, [(f, w) for kk, f, w in early_items if kk == k and f in near]) for k in parts if k not in late_parts]
    extra, late_priors = [], []
    for k in late_parts:
        wheres = [(f, w) for kk, f, w in late_items if kk == k and f in near]
        for kk, f, (at, j) in early_items:
            if kk == k and f in near:
                wheres.append((f, (3 + len(extra), j)))
                extra.append(early[at])
        late_priors.append((k, wheres))
    outs = apply(g, early, prior_m, spans, block_cols, early_items, early_priors)
    params, backup = apply(g, [*got_ab, *extra], prior_m, spans, block_cols, late_items, late_priors, outs)
    return (
        params.reshape(layers, rows, cols),
        new_momentum.reshape(layers, rows, block_cols),
        backup.reshape(layers, rows, block_cols),
    )


def solution(mesh):
    in_specs = (
        P(None, "shard", None),
        P("replica", None, "shard", None),
        P(None, "shard", "replica"),
    )
    out_specs = (P(None, "shard", None), P(None, "shard", "replica"), P(None, "shard", "replica"))
    return jax.shard_map(
        per_device, mesh=mesh, in_specs=in_specs, out_specs=out_specs, check_vma=False
    )
```

```python
import functools

import jax
import jax.numpy as jnp
from jax import lax
from jax.experimental import pallas as pl
from jax.experimental.pallas import tpu as pltpu
from jax.sharding import PartitionSpec as P

D = 8192
LAYERS = 2
KV2 = 2048

outer_beta = 0.9
outer_rate = 0.7
clip_rms = 1.0

grad_gain = outer_rate * (1.0 + outer_beta)
momentum_gain = outer_rate * outer_beta * outer_beta

FLIP = (1, 3, 4)
ORDERS = ((0, 1, 2), (1, 2, 0), (2, 0, 1))


def exchange(value, flip, axis, size):
    return lax.ppermute(value, axis, [(i, i ^ flip) for i in range(size)])


def exchange_two(value, replica_flip, shard_flip):
    pairs = [(r * 16 + s, (r ^ replica_flip) * 16 + (s ^ shard_flip)) for r in range(8) for s in range(16)]
    return lax.ppermute(value, ("replica", "shard"), pairs)


def tie(*values):
    return lax.optimization_barrier(values)


def flip_of(order, bits):
    total = 0
    for edge, bit in zip(order, bits):
        if bit:
            total ^= FLIP[edge]
    return total


def part_rows(rows):
    unit = 16
    tiles = rows // unit
    counts = [tiles // 3 + (1 if k < tiles % 3 else 0) for k in range(3)]
    starts = [sum(counts[:k]) for k in range(3)]
    return [(s * unit, c * unit) for s, c in zip(starts, counts)]


def flips(k, *bits):
    return flip_of(ORDERS[k], bits)


FIRST = ((1, 1, 0), (1, 1, 1))
SECOND = ((1, 0, 0), (1, 0, 1))
KEPT = ((0, 0, 0), (0, 0, 1), (0, 1, 0), (0, 1, 1))


def block_at(own, flip, block_cols):
    return pl.ds(pl.multiple_of((own ^ flip) * block_cols, block_cols), block_cols)


def in_hbm(value):
    return pltpu.with_memory_space_constraint(value, pltpu.HBM)


def drift_kernel(spans, block_cols, items, n_outs, g_ref, r_ref, *rest):
    outs, (g_buf, r_buf, g_sem, r_sem, o_sem) = rest[:n_outs], rest[n_outs:]
    own = lax.axis_index("replica")

    def loads(n):
        k, flip, _, _ = items[n]
        start, count = spans[k]
        place = (pl.ds(start, count), block_at(own, flip, block_cols))
        return (
            pltpu.make_async_copy(g_ref.at[place], g_buf.at[n, pl.ds(0, count)], g_sem.at[n]),
            pltpu.make_async_copy(r_ref.at[place], r_buf.at[n, pl.ds(0, count)], r_sem.at[n]),
        )

    def store(n):
        k, _, out, j = items[n]
        return pltpu.make_async_copy(g_buf.at[n, pl.ds(0, spans[k][1])], outs[out].at[j], o_sem.at[n])

    for n in range(len(items)):
        for copy in loads(n):
            copy.start()
    for n in range(len(items)):
        for copy in loads(n):
            copy.wait()
        count = spans[items[n][0]][1]
        g_buf[n, :count] = g_buf[n, :count] - r_buf[n, :count].astype(jnp.float32)
        store(n).start()
    for n in range(len(items)):
        store(n).wait()


def drift(g, r, spans, block_cols, groups):
    items, shapes = [], []
    for i, group in enumerate(groups):
        for k in range(3):
            shapes.append(jax.ShapeDtypeStruct((len(group), spans[k][1], block_cols), jnp.float32))
        for j, bits in enumerate(group):
            items += [(k, flips(k, *bits), 3 * i + k, j) for k in range(3)]
    most = max(count for _, count in spans)
    n = len(items)
    outs = pl.pallas_call(
        functools.partial(drift_kernel, spans, block_cols, items, len(shapes)),
        out_shape=shapes,
        in_specs=[pl.BlockSpec(memory_space=pltpu.HBM)] * 2,
        out_specs=[pl.BlockSpec(memory_space=pl.ANY)] * len(shapes),
        scratch_shapes=[
            pltpu.VMEM((n, most, block_cols), jnp.float32),
            pltpu.VMEM((n, most, block_cols), jnp.bfloat16),
            pltpu.SemaphoreType.DMA((n,)),
            pltpu.SemaphoreType.DMA((n,)),
            pltpu.SemaphoreType.DMA((n,)),
        ],
        compiler_params=pltpu.CompilerParams(vmem_limit_bytes=10 * 1024 * 1024),
        cost_estimate=pl.CostEstimate(flops=n * most * block_cols, bytes_accessed=10 * n * most * block_cols, transcendentals=0),
        name="drift",
    )(in_hbm(g), in_hbm(r))
    return [outs[3 * i : 3 * i + 3] for i in range(len(groups))]


def apply_kernel(spans, block_cols, items, priors, n_us, before, *refs):
    g_ref, us, (m_ref,) = refs[0], refs[1 : 1 + n_us], refs[1 + n_us : 2 + n_us]
    rest = refs[2 + n_us + before :]
    out_ref, b_ref, g_buf, u_buf, m_buf, v_buf, g_sem, u_sem, m_sem, v_sem, o_sem, b_sem = rest
    own = lax.axis_index("replica")
    back = own ^ lax.rem(own + 7, 8)

    def source(where):
        which, j = where
        return us[which] if j is None else us[which].at[j]

    def loads(n):
        k, flip, where = items[n]
        start, count = spans[k]
        return (
            pltpu.make_async_copy(
                g_ref.at[pl.ds(start, count), block_at(own, flip, block_cols)], g_buf.at[n, pl.ds(0, count)], g_sem.at[n]
            ),
            pltpu.make_async_copy(source(where), u_buf.at[n, pl.ds(0, count)], u_sem.at[n]),
        )

    def store(n):
        k, flip, _ = items[n]
        start, count = spans[k]
        return pltpu.make_async_copy(
            g_buf.at[n, pl.ds(0, count)], out_ref.at[pl.ds(start, count), block_at(own, flip, block_cols)], o_sem.at[n]
        )

    def prior_loads(i):
        k, wheres = priors[i]
        start, count = spans[k]
        m_copy = pltpu.make_async_copy(m_ref.at[pl.ds(start, count)], m_buf.at[i, pl.ds(0, count)], m_sem.at[i])
        v_copies = [
            (flip, pltpu.make_async_copy(source(where), v_buf.at[i, pl.ds(0, count)], v_sem.at[i])) for flip, where in wheres
        ]
        return m_copy, v_copies

    def prior_store(i):
        start, count = spans[priors[i][0]]
        return pltpu.make_async_copy(m_buf.at[i, pl.ds(0, count)], b_ref.at[pl.ds(start, count)], b_sem.at[i])

    for n in range(len(items)):
        for copy in loads(n):
            copy.start()
    for i in range(len(priors)):
        m_copy, v_copies = prior_loads(i)
        m_copy.start()
        for flip, copy in v_copies:
            pl.when(back == flip)(copy.start)
    for n in range(len(items)):
        for copy in loads(n):
            copy.wait()
        count = spans[items[n][0]][1]
        g_buf[n, :count] = g_buf[n, :count] - u_buf[n, :count]
        store(n).start()
    for i in range(len(priors)):
        m_copy, v_copies = prior_loads(i)
        m_copy.wait()
        v_copies[0][1].wait()
        count = spans[priors[i][0]][1]
        m_buf[i, :count] = v_buf[i, :count] * (1.0 / grad_gain) + (outer_beta - momentum_gain / grad_gain) * m_buf[i, :count]
        prior_store(i).start()
    for n in range(len(items)):
        store(n).wait()
    for i in range(len(priors)):
        prior_store(i).wait()


def apply(g, us, prior_m, spans, block_cols, items, priors, before=None):
    most = max(count for _, count in spans)
    n, p = len(items), len(priors)
    operands = [in_hbm(g), *us, prior_m] + ([] if before is None else [in_hbm(b) for b in before])
    hbm, anywhere = pl.BlockSpec(memory_space=pltpu.HBM), pl.BlockSpec(memory_space=pl.ANY)
    return pl.pallas_call(
        functools.partial(apply_kernel, spans, block_cols, items, priors, len(us), 0 if before is None else 2),
        out_shape=[jax.ShapeDtypeStruct(g.shape, jnp.float32), jax.ShapeDtypeStruct(prior_m.shape, jnp.float32)],
        in_specs=[hbm] + [anywhere] * (len(us) + 1) + ([] if before is None else [hbm, hbm]),
        out_specs=[hbm, hbm],
        input_output_aliases={} if before is None else {len(us) + 2: 0, len(us) + 3: 1},
        scratch_shapes=[
            pltpu.VMEM((n, most, block_cols), jnp.float32),
            pltpu.VMEM((n, most, block_cols), jnp.float32),
            pltpu.VMEM((p, most, block_cols), jnp.float32),
            pltpu.VMEM((p, most, block_cols), jnp.float32),
            *[pltpu.SemaphoreType.DMA((count,)) for count in (n, n, p, p, n, p)],
        ],
        compiler_params=pltpu.CompilerParams(vmem_limit_bytes=16 * 1024 * 1024),
        cost_estimate=pl.CostEstimate(flops=n * most * block_cols, bytes_accessed=12 * n * most * block_cols, transcendentals=0),
        name="apply",
    )(*operands)


def clip_factor(square_sum):
    element_count = LAYERS * D * KV2
    rms_value = jnp.sqrt(square_sum / element_count + 1e-06)
    return jnp.minimum(1.0, clip_rms / rms_value)


def per_device(global_params, replica_params, momentum):
    replicas = 8
    layers, rows, cols = global_params.shape
    block_cols = cols // replicas
    g = global_params.reshape(layers * rows, cols)
    r = replica_params.reshape(layers * rows, cols)
    m = momentum.reshape(layers * rows, block_cols)
    spans = part_rows(layers * rows)
    parts = range(3)

    def cross(k, step, value):
        return exchange(value, FLIP[ORDERS[k][step]], "replica", replicas)

    (first,) = drift(g, r, spans, block_cols, [FIRST])
    got1 = [cross(k, 0, first[k]) for k in parts]
    (second,) = drift(g, r, spans, block_cols, [SECOND])
    got2 = [cross(k, 0, second[k]) for k in parts]
    (kept,) = drift(g, r, spans, block_cols, [KEPT])
    third = [kept[k][2:] + got1[k] for k in parts]
    got3 = [cross(k, 1, third[k]) for k in parts]
    fourth = [kept[k][1] + got2[k][1] + got3[k][1] for k in parts]
    got4 = [cross(k, 2, fourth[k]) for k in parts]
    grads = [(kept[k][0] + got2[k][0] + got3[k][0] + got4[k]) / replicas for k in parts]

    squares = jnp.broadcast_to(sum(jnp.sum(p * p, axis=0) for p in grads), (8, block_cols))
    over_y = [exchange_two(squares, a, b) for a, b in ((0, 8), (4, 0), (4, 8))]
    squares = (squares + over_y[0]) + (over_y[1] + over_y[2])
    squares, m = tie(squares, m)
    prior_m = lax.ppermute(m, "replica", [(i, (i + 1) % replicas) for i in range(replicas)])
    for flip in (2, 6, 1):
        squares = squares + exchange(squares, flip, "shard", 16)
    around = [squares]
    for _ in range(3):
        around.append(lax.ppermute(around[-1], "replica", [(i, i // 4 * 4 + (i + 3) % 4) for i in range(replicas)]))
    squares = (around[0] + around[2]) + (around[1] + around[3])
    factor = clip_factor(jnp.broadcast_to(jnp.sum(squares, axis=1, keepdims=True), squares.shape))[:1]
    factor, prior_m = lax.optimization_barrier((factor, prior_m))

    clipped = [p * factor for p in grads]
    mine = [m[start : start + count] for start, count in spans]
    u = [grad_gain * clipped[k] + momentum_gain * mine[k] for k in parts]
    new_momentum = jnp.concatenate([outer_beta * mine[k] + clipped[k] for k in parts])
    got_c = [cross(k, 2, u[k]) for k in parts]
    pair = [jnp.stack([u[k], got_c[k]]) for k in parts]
    got_b = [cross(k, 1, pair[k]) for k in parts]
    pair = list(tie(*pair))
    pair[2], got_b[1] = tie(pair[2], got_b[1])
    got_ac = [cross(k, 0, pair[k]) for k in parts]
    pair[2], got_b[0] = tie(pair[2], got_b[0])
    got_ab = [cross(k, 0, got_b[k]) for k in parts]

    early = [*u, *got_c, *got_b, *got_ac]
    early_at = [
        ((0, 0, 0), 0, None),
        ((0, 0, 1), 3, None),
        ((0, 1, 0), 6, 0),
        ((0, 1, 1), 6, 1),
        ((1, 0, 0), 9, 0),
        ((1, 0, 1), 9, 1),
    ]
    late_at = [((1, 1, 0), 0, 0), ((1, 1, 1), 0, 1)]
    early_items = [(k, flips(k, *bits), (at + k, j)) for bits, at, j in early_at for k in parts]
    late_items = [(k, flips(k, *bits), (at + k, j)) for bits, at, j in late_at for k in parts]
    near = (1, 3, 7)
    late_parts = sorted({k for k, f, _ in late_items if f in near})
    early_priors = [(k, [(f, w) for kk, f, w in early_items if kk == k and f in near]) for k in parts if k not in late_parts]
    extra, late_priors = [], []
    for k in late_parts:
        wheres = [(f, w) for kk, f, w in late_items if kk == k and f in near]
        for kk, f, (at, j) in early_items:
            if kk == k and f in near:
                wheres.append((f, (3 + len(extra), j)))
                extra.append(early[at])
        late_priors.append((k, wheres))
    outs = apply(g, early, prior_m, spans, block_cols, early_items, early_priors)
    params, backup = apply(g, [*got_ab, *extra], prior_m, spans, block_cols, late_items, late_priors, outs)
    return (
        params.reshape(layers, rows, cols),
        new_momentum.reshape(layers, rows, block_cols),
        backup.reshape(layers, rows, block_cols),
    )


def solution(mesh):
    in_specs = (
        P(None, "shard", None),
        P("replica", None, "shard", None),
        P(None, "shard", "replica"),
    )
    out_specs = (P(None, "shard", None), P(None, "shard", "replica"), P(None, "shard", "replica"))
    return jax.shard_map(
        per_device, mesh=mesh, in_specs=in_specs, out_specs=out_specs, check_vma=False
    )
```

```python
import functools

import jax
import jax.numpy as jnp
from jax import lax
from jax.experimental import pallas as pl
from jax.experimental.pallas import tpu as pltpu
from jax.sharding import PartitionSpec as P

D = 8192
LAYERS = 2
KV2 = 2048

outer_beta = 0.9
outer_rate = 0.7
clip_rms = 1.0

grad_gain = outer_rate * (1.0 + outer_beta)
momentum_gain = outer_rate * outer_beta * outer_beta

FLIP = (1, 3, 4)
ORDERS = ((0, 1, 2), (1, 2, 0), (2, 0, 1))


def exchange(value, flip, axis, size):
    return lax.ppermute(value, axis, [(i, i ^ flip) for i in range(size)])


def exchange_two(value, replica_flip, shard_flip):
    pairs = [(r * 16 + s, (r ^ replica_flip) * 16 + (s ^ shard_flip)) for r in range(8) for s in range(16)]
    return lax.ppermute(value, ("replica", "shard"), pairs)


def tie(*values):
    return lax.optimization_barrier(values)


def flip_of(order, bits):
    total = 0
    for edge, bit in zip(order, bits):
        if bit:
            total ^= FLIP[edge]
    return total


def part_rows(rows):
    unit = 16
    tiles = rows // unit
    counts = [tiles // 3 + (1 if k < tiles % 3 else 0) for k in range(3)]
    starts = [sum(counts[:k]) for k in range(3)]
    return [(s * unit, c * unit) for s, c in zip(starts, counts)]


def flips(k, *bits):
    return flip_of(ORDERS[k], bits)


FIRST = ((1, 1, 0), (1, 1, 1))
SECOND = ((1, 0, 0), (1, 0, 1))
KEPT = ((0, 0, 0), (0, 0, 1), (0, 1, 0), (0, 1, 1))


def block_at(own, flip, block_cols):
    return pl.ds(pl.multiple_of((own ^ flip) * block_cols, block_cols), block_cols)


def in_hbm(value):
    return pltpu.with_memory_space_constraint(value, pltpu.HBM)


def drift_kernel(spans, block_cols, items, n_outs, g_ref, r_ref, *rest):
    outs, (g_buf, r_buf, g_sem, r_sem, o_sem) = rest[:n_outs], rest[n_outs:]
    own = lax.axis_index("replica")

    def loads(n):
        k, flip, _, _ = items[n]
        start, count = spans[k]
        place = (pl.ds(start, count), block_at(own, flip, block_cols))
        return (
            pltpu.make_async_copy(g_ref.at[place], g_buf.at[n, pl.ds(0, count)], g_sem.at[n]),
            pltpu.make_async_copy(r_ref.at[place], r_buf.at[n, pl.ds(0, count)], r_sem.at[n]),
        )

    def store(n):
        k, _, out, j = items[n]
        return pltpu.make_async_copy(g_buf.at[n, pl.ds(0, spans[k][1])], outs[out].at[j], o_sem.at[n])

    for n in range(len(items)):
        for copy in loads(n):
            copy.start()
    for n in range(len(items)):
        for copy in loads(n):
            copy.wait()
        count = spans[items[n][0]][1]
        g_buf[n, :count] = g_buf[n, :count] - r_buf[n, :count].astype(jnp.float32)
        store(n).start()
    for n in range(len(items)):
        store(n).wait()


def drift(g, r, spans, block_cols, groups):
    items, shapes = [], []
    for i, group in enumerate(groups):
        for k in range(3):
            shapes.append(jax.ShapeDtypeStruct((len(group), spans[k][1], block_cols), jnp.float32))
        for j, bits in enumerate(group):
            items += [(k, flips(k, *bits), 3 * i + k, j) for k in range(3)]
    most = max(count for _, count in spans)
    n = len(items)
    outs = pl.pallas_call(
        functools.partial(drift_kernel, spans, block_cols, items, len(shapes)),
        out_shape=shapes,
        in_specs=[pl.BlockSpec(memory_space=pltpu.HBM)] * 2,
        out_specs=[pl.BlockSpec(memory_space=pl.ANY)] * len(shapes),
        scratch_shapes=[
            pltpu.VMEM((n, most, block_cols), jnp.float32),
            pltpu.VMEM((n, most, block_cols), jnp.bfloat16),
            pltpu.SemaphoreType.DMA((n,)),
            pltpu.SemaphoreType.DMA((n,)),
            pltpu.SemaphoreType.DMA((n,)),
        ],
        compiler_params=pltpu.CompilerParams(vmem_limit_bytes=10 * 1024 * 1024),
        cost_estimate=pl.CostEstimate(flops=n * most * block_cols, bytes_accessed=10 * n * most * block_cols, transcendentals=0),
        name="drift",
    )(in_hbm(g), in_hbm(r))
    return [outs[3 * i : 3 * i + 3] for i in range(len(groups))]


def apply_kernel(spans, block_cols, items, priors, n_us, before, *refs):
    g_ref, us, (m_ref,) = refs[0], refs[1 : 1 + n_us], refs[1 + n_us : 2 + n_us]
    rest = refs[2 + n_us + before :]
    out_ref, b_ref, g_buf, u_buf, m_buf, v_buf, g_sem, u_sem, m_sem, v_sem, o_sem, b_sem = rest
    own = lax.axis_index("replica")
    back = own ^ lax.rem(own + 7, 8)

    def source(where):
        which, j = where
        return us[which] if j is None else us[which].at[j]

    def loads(n):
        k, flip, where = items[n]
        start, count = spans[k]
        return (
            pltpu.make_async_copy(
                g_ref.at[pl.ds(start, count), block_at(own, flip, block_cols)], g_buf.at[n, pl.ds(0, count)], g_sem.at[n]
            ),
            pltpu.make_async_copy(source(where), u_buf.at[n, pl.ds(0, count)], u_sem.at[n]),
        )

    def store(n):
        k, flip, _ = items[n]
        start, count = spans[k]
        return pltpu.make_async_copy(
            g_buf.at[n, pl.ds(0, count)], out_ref.at[pl.ds(start, count), block_at(own, flip, block_cols)], o_sem.at[n]
        )

    def prior_loads(i):
        k, wheres = priors[i]
        start, count = spans[k]
        m_copy = pltpu.make_async_copy(m_ref.at[pl.ds(start, count)], m_buf.at[i, pl.ds(0, count)], m_sem.at[i])
        v_copies = [
            (flip, pltpu.make_async_copy(source(where), v_buf.at[i, pl.ds(0, count)], v_sem.at[i])) for flip, where in wheres
        ]
        return m_copy, v_copies

    def prior_store(i):
        start, count = spans[priors[i][0]]
        return pltpu.make_async_copy(m_buf.at[i, pl.ds(0, count)], b_ref.at[pl.ds(start, count)], b_sem.at[i])

    for n in range(len(items)):
        for copy in loads(n):
            copy.start()
    for i in range(len(priors)):
        m_copy, v_copies = prior_loads(i)
        m_copy.start()
        for flip, copy in v_copies:
            pl.when(back == flip)(copy.start)
    for n in range(len(items)):
        for copy in loads(n):
            copy.wait()
        count = spans[items[n][0]][1]
        g_buf[n, :count] = g_buf[n, :count] - u_buf[n, :count]
        store(n).start()
    for i in range(len(priors)):
        m_copy, v_copies = prior_loads(i)
        m_copy.wait()
        v_copies[0][1].wait()
        count = spans[priors[i][0]][1]
        m_buf[i, :count] = v_buf[i, :count] * (1.0 / grad_gain) + (outer_beta - momentum_gain / grad_gain) * m_buf[i, :count]
        prior_store(i).start()
    for n in range(len(items)):
        store(n).wait()
    for i in range(len(priors)):
        prior_store(i).wait()


def apply(g, us, prior_m, spans, block_cols, items, priors, before=None):
    most = max(count for _, count in spans)
    n, p = len(items), len(priors)
    operands = [in_hbm(g), *us, prior_m] + ([] if before is None else [in_hbm(b) for b in before])
    hbm, anywhere = pl.BlockSpec(memory_space=pltpu.HBM), pl.BlockSpec(memory_space=pl.ANY)
    return pl.pallas_call(
        functools.partial(apply_kernel, spans, block_cols, items, priors, len(us), 0 if before is None else 2),
        out_shape=[jax.ShapeDtypeStruct(g.shape, jnp.float32), jax.ShapeDtypeStruct(prior_m.shape, jnp.float32)],
        in_specs=[hbm] + [anywhere] * (len(us) + 1) + ([] if before is None else [hbm, hbm]),
        out_specs=[hbm, hbm],
        input_output_aliases={} if before is None else {len(us) + 2: 0, len(us) + 3: 1},
        scratch_shapes=[
            pltpu.VMEM((n, most, block_cols), jnp.float32),
            pltpu.VMEM((n, most, block_cols), jnp.float32),
            pltpu.VMEM((p, most, block_cols), jnp.float32),
            pltpu.VMEM((p, most, block_cols), jnp.float32),
            *[pltpu.SemaphoreType.DMA((count,)) for count in (n, n, p, p, n, p)],
        ],
        compiler_params=pltpu.CompilerParams(vmem_limit_bytes=16 * 1024 * 1024),
        cost_estimate=pl.CostEstimate(flops=n * most * block_cols, bytes_accessed=12 * n * most * block_cols, transcendentals=0),
        name="apply",
    )(*operands)


def clip_factor(square_sum):
    element_count = LAYERS * D * KV2
    rms_value = jnp.sqrt(square_sum / element_count + 1e-06)
    return jnp.minimum(1.0, clip_rms / rms_value)


def per_device(global_params, replica_params, momentum):
    replicas = 8
    layers, rows, cols = global_params.shape
    block_cols = cols // replicas
    g = global_params.reshape(layers * rows, cols)
    r = replica_params.reshape(layers * rows, cols)
    m = momentum.reshape(layers * rows, block_cols)
    spans = part_rows(layers * rows)
    parts = range(3)

    def cross(k, step, value):
        return exchange(value, FLIP[ORDERS[k][step]], "replica", replicas)

    (first,) = drift(g, r, spans, block_cols, [FIRST])
    got1 = [cross(k, 0, first[k]) for k in parts]
    (second,) = drift(g, r, spans, block_cols, [SECOND])
    got2 = [cross(k, 0, second[k]) for k in parts]
    (kept,) = drift(g, r, spans, block_cols, [KEPT])
    third = [kept[k][2:] + got1[k] for k in parts]
    got3 = [cross(k, 1, third[k]) for k in parts]
    fourth = [kept[k][1] + got2[k][1] + got3[k][1] for k in parts]
    got4 = [cross(k, 2, fourth[k]) for k in parts]
    grads = [(kept[k][0] + got2[k][0] + got3[k][0] + got4[k]) / replicas for k in parts]

    squares = sum(jnp.sum(p * p, axis=0) for p in grads)
    squares = jnp.broadcast_to(squares[:128] + squares[128:], (8, 128))
    over_y = [exchange_two(squares, a, b) for a, b in ((0, 8), (4, 0), (4, 8))]
    squares = (squares + over_y[0]) + (over_y[1] + over_y[2])
    squares, m = tie(squares, m)
    prior_m = lax.ppermute(m, "replica", [(i, (i + 1) % replicas) for i in range(replicas)])
    for flip in (2, 6, 1):
        squares = squares + exchange(squares, flip, "shard", 16)
    around = [squares]
    for _ in range(3):
        around.append(lax.ppermute(around[-1], "replica", [(i, i // 4 * 4 + (i + 3) % 4) for i in range(replicas)]))
    squares = (around[0] + around[2]) + (around[1] + around[3])
    factor = clip_factor(jnp.broadcast_to(jnp.sum(squares, axis=1, keepdims=True), (8, block_cols)))[:1]
    factor, prior_m = lax.optimization_barrier((factor, prior_m))

    clipped = [p * factor for p in grads]
    mine = [m[start : start + count] for start, count in spans]
    u = [grad_gain * clipped[k] + momentum_gain * mine[k] for k in parts]
    new_momentum = jnp.concatenate([outer_beta * mine[k] + clipped[k] for k in parts])
    got_c = [cross(k, 2, u[k]) for k in parts]
    pair = [jnp.stack([u[k], got_c[k]]) for k in parts]
    got_b = [cross(k, 1, pair[k]) for k in parts]
    pair = list(tie(*pair))
    pair[2], got_b[1] = tie(pair[2], got_b[1])
    got_ac = [cross(k, 0, pair[k]) for k in parts]
    pair[2], got_b[0] = tie(pair[2], got_b[0])
    got_ab = [cross(k, 0, got_b[k]) for k in parts]

    early = [*u, *got_c, *got_b, *got_ac]
    early_at = [
        ((0, 0, 0), 0, None),
        ((0, 0, 1), 3, None),
        ((0, 1, 0), 6, 0),
        ((0, 1, 1), 6, 1),
        ((1, 0, 0), 9, 0),
        ((1, 0, 1), 9, 1),
    ]
    late_at = [((1, 1, 0), 0, 0), ((1, 1, 1), 0, 1)]
    early_items = [(k, flips(k, *bits), (at + k, j)) for bits, at, j in early_at for k in parts]
    late_items = [(k, flips(k, *bits), (at + k, j)) for bits, at, j in late_at for k in parts]
    near = (1, 3, 7)
    late_parts = sorted({k for k, f, _ in late_items if f in near})
    early_priors = [(k, [(f, w) for kk, f, w in early_items if kk == k and f in near]) for k in parts if k not in late_parts]
    extra, late_priors = [], []
    for k in late_parts:
        wheres = [(f, w) for kk, f, w in late_items if kk == k and f in near]
        for kk, f, (at, j) in early_items:
            if kk == k and f in near:
                wheres.append((f, (3 + len(extra), j)))
                extra.append(early[at])
        late_priors.append((k, wheres))
    outs = apply(g, early, prior_m, spans, block_cols, early_items, early_priors)
    params, backup = apply(g, [*got_ab, *extra], prior_m, spans, block_cols, late_items, late_priors, outs)
    return (
        params.reshape(layers, rows, cols),
        new_momentum.reshape(layers, rows, block_cols),
        backup.reshape(layers, rows, block_cols),
    )


def solution(mesh):
    in_specs = (
        P(None, "shard", None),
        P("replica", None, "shard", None),
        P(None, "shard", "replica"),
    )
    out_specs = (P(None, "shard", None), P(None, "shard", "replica"), P(None, "shard", "replica"))
    return jax.shard_map(
        per_device, mesh=mesh, in_specs=in_specs, out_specs=out_specs, check_vma=False
    )
```

```python
import functools

import jax
import jax.numpy as jnp
from jax import lax
from jax.experimental import pallas as pl
from jax.experimental.pallas import tpu as pltpu
from jax.sharding import PartitionSpec as P

D = 8192
LAYERS = 2
KV2 = 2048

outer_beta = 0.9
outer_rate = 0.7
clip_rms = 1.0

grad_gain = outer_rate * (1.0 + outer_beta)
momentum_gain = outer_rate * outer_beta * outer_beta

FLIP = (1, 3, 4)
ORDERS = ((0, 1, 2), (1, 2, 0), (2, 0, 1))


def exchange(value, flip, axis, size):
    return lax.ppermute(value, axis, [(i, i ^ flip) for i in range(size)])


def exchange_two(value, replica_flip, shard_flip):
    pairs = [(r * 16 + s, (r ^ replica_flip) * 16 + (s ^ shard_flip)) for r in range(8) for s in range(16)]
    return lax.ppermute(value, ("replica", "shard"), pairs)


def tie(*values):
    return lax.optimization_barrier(values)


def flip_of(order, bits):
    total = 0
    for edge, bit in zip(order, bits):
        if bit:
            total ^= FLIP[edge]
    return total


def part_rows(rows):
    unit = 16
    tiles = rows // unit
    counts = [tiles // 3 + (1 if k < tiles % 3 else 0) for k in range(3)]
    starts = [sum(counts[:k]) for k in range(3)]
    return [(s * unit, c * unit) for s, c in zip(starts, counts)]


def flips(k, *bits):
    return flip_of(ORDERS[k], bits)


FIRST = ((1, 1, 0), (1, 1, 1), (1, 0, 1))
SECOND = ((1, 0, 0),)
KEPT = ((0, 0, 0), (0, 0, 1), (0, 1, 0), (0, 1, 1))


def block_at(own, flip, block_cols):
    return pl.ds(pl.multiple_of((own ^ flip) * block_cols, block_cols), block_cols)


def in_hbm(value):
    return pltpu.with_memory_space_constraint(value, pltpu.HBM)


def drift_kernel(spans, block_cols, items, n_outs, g_ref, r_ref, *rest):
    outs, (g_buf, r_buf, g_sem, r_sem, o_sem) = rest[:n_outs], rest[n_outs:]
    own = lax.axis_index("replica")

    def loads(n):
        k, flip, _, _ = items[n]
        start, count = spans[k]
        place = (pl.ds(start, count), block_at(own, flip, block_cols))
        return (
            pltpu.make_async_copy(g_ref.at[place], g_buf.at[n, pl.ds(0, count)], g_sem.at[n]),
            pltpu.make_async_copy(r_ref.at[place], r_buf.at[n, pl.ds(0, count)], r_sem.at[n]),
        )

    def store(n):
        k, _, out, j = items[n]
        return pltpu.make_async_copy(g_buf.at[n, pl.ds(0, spans[k][1])], outs[out].at[j], o_sem.at[n])

    for n in range(len(items)):
        for copy in loads(n):
            copy.start()
    for n in range(len(items)):
        for copy in loads(n):
            copy.wait()
        count = spans[items[n][0]][1]
        g_buf[n, :count] = g_buf[n, :count] - r_buf[n, :count].astype(jnp.float32)
        store(n).start()
    for n in range(len(items)):
        store(n).wait()


def drift(g, r, spans, block_cols, groups):
    items, shapes = [], []
    for i, group in enumerate(groups):
        for k in range(3):
            shapes.append(jax.ShapeDtypeStruct((len(group), spans[k][1], block_cols), jnp.float32))
        for j, bits in enumerate(group):
            items += [(k, flips(k, *bits), 3 * i + k, j) for k in range(3)]
    most = max(count for _, count in spans)
    n = len(items)
    outs = pl.pallas_call(
        functools.partial(drift_kernel, spans, block_cols, items, len(shapes)),
        out_shape=shapes,
        in_specs=[pl.BlockSpec(memory_space=pltpu.HBM)] * 2,
        out_specs=[pl.BlockSpec(memory_space=pl.ANY)] * len(shapes),
        scratch_shapes=[
            pltpu.VMEM((n, most, block_cols), jnp.float32),
            pltpu.VMEM((n, most, block_cols), jnp.bfloat16),
            pltpu.SemaphoreType.DMA((n,)),
            pltpu.SemaphoreType.DMA((n,)),
            pltpu.SemaphoreType.DMA((n,)),
        ],
        compiler_params=pltpu.CompilerParams(vmem_limit_bytes=10 * 1024 * 1024),
        cost_estimate=pl.CostEstimate(flops=n * most * block_cols, bytes_accessed=10 * n * most * block_cols, transcendentals=0),
        name="drift",
    )(in_hbm(g), in_hbm(r))
    return [outs[3 * i : 3 * i + 3] for i in range(len(groups))]


def apply_kernel(spans, block_cols, items, priors, n_us, before, *refs):
    g_ref, us, (m_ref,) = refs[0], refs[1 : 1 + n_us], refs[1 + n_us : 2 + n_us]
    rest = refs[2 + n_us + before :]
    out_ref, b_ref, g_buf, u_buf, m_buf, v_buf, g_sem, u_sem, m_sem, v_sem, o_sem, b_sem = rest
    own = lax.axis_index("replica")
    back = own ^ lax.rem(own + 7, 8)

    def source(where):
        which, j = where
        return us[which] if j is None else us[which].at[j]

    def loads(n):
        k, flip, where = items[n]
        start, count = spans[k]
        return (
            pltpu.make_async_copy(
                g_ref.at[pl.ds(start, count), block_at(own, flip, block_cols)], g_buf.at[n, pl.ds(0, count)], g_sem.at[n]
            ),
            pltpu.make_async_copy(source(where), u_buf.at[n, pl.ds(0, count)], u_sem.at[n]),
        )

    def store(n):
        k, flip, _ = items[n]
        start, count = spans[k]
        return pltpu.make_async_copy(
            g_buf.at[n, pl.ds(0, count)], out_ref.at[pl.ds(start, count), block_at(own, flip, block_cols)], o_sem.at[n]
        )

    def prior_loads(i):
        k, wheres = priors[i]
        start, count = spans[k]
        m_copy = pltpu.make_async_copy(m_ref.at[pl.ds(start, count)], m_buf.at[i, pl.ds(0, count)], m_sem.at[i])
        v_copies = [
            (flip, pltpu.make_async_copy(source(where), v_buf.at[i, pl.ds(0, count)], v_sem.at[i])) for flip, where in wheres
        ]
        return m_copy, v_copies

    def prior_store(i):
        start, count = spans[priors[i][0]]
        return pltpu.make_async_copy(m_buf.at[i, pl.ds(0, count)], b_ref.at[pl.ds(start, count)], b_sem.at[i])

    for n in range(len(items)):
        for copy in loads(n):
            copy.start()
    for i in range(len(priors)):
        m_copy, v_copies = prior_loads(i)
        m_copy.start()
        for flip, copy in v_copies:
            pl.when(back == flip)(copy.start)
    for n in range(len(items)):
        for copy in loads(n):
            copy.wait()
        count = spans[items[n][0]][1]
        g_buf[n, :count] = g_buf[n, :count] - u_buf[n, :count]
        store(n).start()
    for i in range(len(priors)):
        m_copy, v_copies = prior_loads(i)
        m_copy.wait()
        v_copies[0][1].wait()
        count = spans[priors[i][0]][1]
        m_buf[i, :count] = v_buf[i, :count] * (1.0 / grad_gain) + (outer_beta - momentum_gain / grad_gain) * m_buf[i, :count]
        prior_store(i).start()
    for n in range(len(items)):
        store(n).wait()
    for i in range(len(priors)):
        prior_store(i).wait()


def apply(g, us, prior_m, spans, block_cols, items, priors, before=None):
    most = max(count for _, count in spans)
    n, p = len(items), len(priors)
    operands = [in_hbm(g), *us, prior_m] + ([] if before is None else [in_hbm(b) for b in before])
    hbm, anywhere = pl.BlockSpec(memory_space=pltpu.HBM), pl.BlockSpec(memory_space=pl.ANY)
    return pl.pallas_call(
        functools.partial(apply_kernel, spans, block_cols, items, priors, len(us), 0 if before is None else 2),
        out_shape=[jax.ShapeDtypeStruct(g.shape, jnp.float32), jax.ShapeDtypeStruct(prior_m.shape, jnp.float32)],
        in_specs=[hbm] + [anywhere] * (len(us) + 1) + ([] if before is None else [hbm, hbm]),
        out_specs=[hbm, hbm],
        input_output_aliases={} if before is None else {len(us) + 2: 0, len(us) + 3: 1},
        scratch_shapes=[
            pltpu.VMEM((n, most, block_cols), jnp.float32),
            pltpu.VMEM((n, most, block_cols), jnp.float32),
            pltpu.VMEM((p, most, block_cols), jnp.float32),
            pltpu.VMEM((p, most, block_cols), jnp.float32),
            *[pltpu.SemaphoreType.DMA((count,)) for count in (n, n, p, p, n, p)],
        ],
        compiler_params=pltpu.CompilerParams(vmem_limit_bytes=16 * 1024 * 1024),
        cost_estimate=pl.CostEstimate(flops=n * most * block_cols, bytes_accessed=12 * n * most * block_cols, transcendentals=0),
        name="apply",
    )(*operands)


def clip_factor(square_sum):
    element_count = LAYERS * D * KV2
    rms_value = jnp.sqrt(square_sum / element_count + 1e-06)
    return jnp.minimum(1.0, clip_rms / rms_value)


def per_device(global_params, replica_params, momentum):
    replicas = 8
    layers, rows, cols = global_params.shape
    block_cols = cols // replicas
    g = global_params.reshape(layers * rows, cols)
    r = replica_params.reshape(layers * rows, cols)
    m = momentum.reshape(layers * rows, block_cols)
    spans = part_rows(layers * rows)
    parts = range(3)

    def cross(k, step, value):
        return exchange(value, FLIP[ORDERS[k][step]], "replica", replicas)

    (first,) = drift(g, r, spans, block_cols, [FIRST])
    got1 = [cross(k, 0, first[k]) for k in parts]
    second, kept = drift(g, r, spans, block_cols, [SECOND, KEPT])
    third = [kept[k][2:] + got1[k][:2] for k in parts]
    got3 = [cross(k, 1, third[k]) for k in parts]
    got2 = [cross(k, 0, second[k][0]) for k in parts]
    fourth = [kept[k][1] + got1[k][2] + got3[k][1] for k in parts]
    got4 = [cross(k, 2, fourth[k]) for k in parts]
    grads = [(kept[k][0] + got2[k] + got3[k][0] + got4[k]) / replicas for k in parts]

    squares = sum(jnp.sum(p * p, axis=0) for p in grads)
    squares = jnp.broadcast_to(squares[:128] + squares[128:], (8, 128))
    over_y = [exchange_two(squares, a, b) for a, b in ((0, 8), (4, 0), (4, 8))]
    squares = (squares + over_y[0]) + (over_y[1] + over_y[2])
    squares, m = tie(squares, m)
    prior_m = lax.ppermute(m, "replica", [(i, (i + 1) % replicas) for i in range(replicas)])
    for flip in (2, 6, 1):
        squares = squares + exchange(squares, flip, "shard", 16)
    around = [squares]
    for _ in range(3):
        around.append(lax.ppermute(around[-1], "replica", [(i, i // 4 * 4 + (i + 3) % 4) for i in range(replicas)]))
    squares = (around[0] + around[2]) + (around[1] + around[3])
    factor = clip_factor(jnp.broadcast_to(jnp.sum(squares, axis=1, keepdims=True), (8, block_cols)))[:1]
    factor, prior_m = lax.optimization_barrier((factor, prior_m))

    clipped = [p * factor for p in grads]
    mine = [m[start : start + count] for start, count in spans]
    u = [grad_gain * clipped[k] + momentum_gain * mine[k] for k in parts]
    new_momentum = jnp.concatenate([outer_beta * mine[k] + clipped[k] for k in parts])
    got_c = [cross(k, 2, u[k]) for k in parts]
    pair = [jnp.stack([u[k], got_c[k]]) for k in parts]
    got_b = [cross(k, 1, pair[k]) for k in parts]
    pair = list(tie(*pair))
    pair[2], got_b[1] = tie(pair[2], got_b[1])
    got_ac = [cross(k, 0, pair[k]) for k in parts]
    pair[2], got_b[0] = tie(pair[2], got_b[0])
    got_ab = [cross(k, 0, got_b[k]) for k in parts]

    early = [*u, *got_c, *got_b, *got_ac]
    early_at = [
        ((0, 0, 0), 0, None),
        ((0, 0, 1), 3, None),
        ((0, 1, 0), 6, 0),
        ((0, 1, 1), 6, 1),
        ((1, 0, 0), 9, 0),
        ((1, 0, 1), 9, 1),
    ]
    late_at = [((1, 1, 0), 0, 0), ((1, 1, 1), 0, 1)]
    early_items = [(k, flips(k, *bits), (at + k, j)) for bits, at, j in early_at for k in parts]
    late_items = [(k, flips(k, *bits), (at + k, j)) for bits, at, j in late_at for k in parts]
    near = (1, 3, 7)
    late_parts = sorted({k for k, f, _ in late_items if f in near})
    early_priors = [(k, [(f, w) for kk, f, w in early_items if kk == k and f in near]) for k in parts if k not in late_parts]
    extra, late_priors = [], []
    for k in late_parts:
        wheres = [(f, w) for kk, f, w in late_items if kk == k and f in near]
        for kk, f, (at, j) in early_items:
            if kk == k and f in near:
                wheres.append((f, (3 + len(extra), j)))
                extra.append(early[at])
        late_priors.append((k, wheres))
    outs = apply(g, early, prior_m, spans, block_cols, early_items, early_priors)
    params, backup = apply(g, [*got_ab, *extra], prior_m, spans, block_cols, late_items, late_priors, outs)
    return (
        params.reshape(layers, rows, cols),
        new_momentum.reshape(layers, rows, block_cols),
        backup.reshape(layers, rows, block_cols),
    )


def solution(mesh):
    in_specs = (
        P(None, "shard", None),
        P("replica", None, "shard", None),
        P(None, "shard", "replica"),
    )
    out_specs = (P(None, "shard", None), P(None, "shard", "replica"), P(None, "shard", "replica"))
    return jax.shard_map(
        per_device, mesh=mesh, in_specs=in_specs, out_specs=out_specs, check_vma=False
    )
```
